128 devices in a mesh: rep: 16 (over z_lo, y, core), tp: 8 (over z_hi, x).
Axes of the slice: x: 4, y: 4, z: 4 (z_hi: 2, z_lo: 2; z = z_hi * 2 + z_lo), core: 2. Of those that a mesh axis runs over, the one named last changes fastest.
Arguments:
- tokens: bfloat16 [16384, 4608], P('rep'), may hold values from -5 to 5
- gain_pre: float32 [4608], replicated, may hold values from 0.5 to 1.5
- gain_post: float32 [4608], replicated, may hold values from 0.5 to 1.5
- qkv_shards: bfloat16 [16, 4608, 256], P('rep', 'tp'), may hold values from -0.5 to 0.5
- out_shards: bfloat16 [16, 128, 4608], P('rep', None, 'tp'), may hold values from -0.125 to 0.125
- shard_map: int32 [16], replicated, may hold values from 0 to 15, as said below
- positions: int32 [16384], P('rep'), may hold values from 0 to 1023, as said below
Outputs:
- layer_out: bfloat16 [16384, 4608], P('rep')
The draws below stay inside these ranges and needn't reach their ends.
Inputs may be any that keep to these rules, and one draw needn't show every extreme that they name: `shard_map`: each of 0 to 15 appears exactly once. Within each aligned block of 1024 tokens the positions start at 0 and each next position is one more than the one before or 0; the first block holds one document.
All inputs are finite; a program needn't handle non-finite values.
Results may differ from the reference program's by a relative error of at most 0.019.
Values may be sent and summed in bfloat16 or wider, within the bound.
A program may use at most 128 MiB of HBM per device.

```python
import math
import jax
import jax.numpy as jnp
from jax import lax

D = 4608
HEADS = 16
KVH = 8
HDIM = 128
TOK_DEV = 1024
TOKENS = 16384
BLOCK_COLS = 256
HEAD_ROWS = 128
N_REP = 16
N_TP = 8


def shard_order(key):
    return jax.random.permutation(jax.random.fold_in(key, 101), N_REP).astype(jnp.int32)


def draw_shard_map(key, part):
    return shard_order(key)


def draw_qkv_shards(key, part):
    order = shard_order(key)
    key = jax.random.fold_in(key, 7)
    per_group = HEADS // KVH
    base = jnp.clip(jax.random.normal(key, (D, KVH, per_group + 2, HDIM), jnp.float32), -6.0, 6.0) * D ** (-0.5)
    logical = jnp.clip(base.reshape(D, N_REP, BLOCK_COLS), -0.5, 0.5)
    return jnp.transpose(logical[:, order, :], (1, 0, 2)).astype(jnp.bfloat16)


def draw_tokens(key, part):
    key = jax.random.fold_in(key, 3)
    noise_key, row_key, col_key = jax.random.split(key, 3)
    noise_part = jnp.clip(jax.random.normal(noise_key, (TOKENS, D), jnp.float32), -5.0, 5.0)
    row_scale = jnp.exp(jax.random.uniform(row_key, (TOKENS, 1), jnp.float32, -2.3, 0.0))
    col_scale = jnp.exp(jax.random.uniform(col_key, (1, D), jnp.float32, -2.3, 0.0))
    return (noise_part * row_scale * col_scale).astype(jnp.bfloat16)


def draw_positions(key, part):
    key = jax.random.fold_in(key, 5)
    row_index = jnp.arange(TOKENS, dtype=jnp.int32)
    restart = jax.random.randint(key, (TOKENS,), 0, max(TOK_DEV // 4, 2)) == 0
    restart = jnp.logical_or(restart, row_index % TOK_DEV == 0)
    restart = jnp.where(row_index < TOK_DEV, row_index == 0, restart)
    latest = lax.cummax(jnp.where(restart, row_index, 0), axis=0)
    return (row_index - latest).astype(jnp.int32)


def levels(rng, dims, cuts, low, high):
    def one(axis_at, shards_of):
        draws = jax.random.uniform(jax.random.fold_in(jax.random.fold_in(rng, 6), axis_at), (shards_of,), jnp.float32, low / len(cuts), high / len(cuts))
        return jnp.repeat(jnp.exp(draws), dims[axis_at] // shards_of).reshape((-1,) + (1,) * (len(dims) - axis_at - 1))

    loudness = one(*cuts[0])
    for cut in cuts[1:]:
        loudness = loudness * one(*cut)
    return loudness


def noise(stream_key, dims, scale, bound, shards=(), held_as=jnp.bfloat16):
    entries = scale * jax.random.normal(stream_key, dims, jnp.float32)
    if shards:
        entries = entries * levels(stream_key, dims, shards, -0.22, 0.18)
    return jnp.clip(entries, -bound, bound).astype(held_as)


def setup_inputs(seed: int = 0) -> dict:
    seeds = jax.random.split(jax.random.key(seed), 8)
    return {
        "tokens": draw_tokens(jax.random.fold_in(seeds[7], 71), 0),
        "gain_pre": jnp.clip(1.0 + 0.1 * jax.random.normal(seeds[1], (D,), jnp.float32), 0.5, 1.5),
        "gain_post": jnp.clip(1.0 + 0.1 * jax.random.normal(seeds[2], (D,), jnp.float32), 0.5, 1.5),
        "qkv_shards": draw_qkv_shards(jax.random.fold_in(seeds[7], 71), 0),
        "out_shards": noise(seeds[4], (N_REP, HEAD_ROWS, D), (HEADS * HDIM) ** -0.5, 0.125, ((0, 16), (2, 8))),
        "shard_map": draw_shard_map(jax.random.fold_in(seeds[7], 71), 0),
        "positions": draw_positions(jax.random.fold_in(seeds[7], 71), 0),
    }


QUERY_SCALE = 1.0 / 12.0
EPS = 1e-06

def rotate(values, positions):
    half_dim = values.shape[-1] // 2
    freq_index = jnp.arange(half_dim, dtype=jnp.float32)
    frequency = jnp.exp(freq_index * (-2.0 * math.log(10000.0) / values.shape[-1]))
    angles = positions.astype(jnp.float32)[:, None] * frequency[None, :]
    shape_out = (values.shape[0],) + (1,) * (values.ndim - 2) + (half_dim,)
    cosine = jnp.cos(angles).reshape(shape_out)
    sine_part = jnp.sin(angles).reshape(shape_out)
    lower_half = values[..., :half_dim]
    upper_half = values[..., half_dim:]
    return jnp.concatenate([lower_half * cosine - upper_half * sine_part, upper_half * cosine + lower_half * sine_part], axis=-1)

def attend(projected, positions):
    row_count = projected.shape[0]
    per_group = HEADS // KVH
    groups = projected.reshape(row_count, -1, (per_group + 2) * HDIM)
    queries = groups[:, :, :per_group * HDIM].reshape(row_count, -1, per_group, HDIM)
    key_rows = groups[:, :, per_group * HDIM:(per_group + 1) * HDIM]
    value_rows = groups[:, :, (per_group + 1) * HDIM:]
    queries = (rotate(queries, positions) * QUERY_SCALE).astype(jnp.bfloat16)
    key_rows = rotate(key_rows, positions).astype(jnp.bfloat16)
    value_rows = value_rows.astype(jnp.bfloat16)
    scores = jnp.einsum('tgqd,sgd->gqts', queries.astype(jnp.float32), key_rows.astype(jnp.float32))
    row_index = jnp.arange(row_count, dtype=jnp.int32)
    allowed = (row_index[None, :] <= row_index[:, None]) & (row_index[None, :] >= row_index[:, None] - positions[:, None])
    scores = jnp.where(allowed, scores, -1e+30)
    row_max = lax.optimization_barrier(jnp.max(scores, axis=-1, keepdims=True))
    powers = jnp.exp(scores - row_max)
    row_total = lax.optimization_barrier(jnp.sum(powers, axis=-1, keepdims=True))
    attn_weights = (powers / row_total).astype(jnp.bfloat16)
    head_out = jnp.einsum('gqts,sgd->tgqd', attn_weights.astype(jnp.float32), value_rows.astype(jnp.float32))
    return head_out.astype(jnp.bfloat16).reshape(row_count, -1)

def reference(tokens, gain_pre, gain_post, qkv_shards, out_shards, shard_map, positions):
    order = jnp.arange(N_REP, dtype=jnp.int32)
    inverse = lax.optimization_barrier(jnp.sum(jnp.where(shard_map[:, None] == order[None, :], order[:, None], 0), axis=0)).astype(jnp.int32)
    qkv_weight = jnp.transpose(jnp.take(qkv_shards, inverse, axis=0), (1, 0, 2)).reshape(D, -1)
    out_weight = jnp.take(out_shards, inverse, axis=0).reshape(-1, D)
    row_span = out_weight.shape[0] // N_TP

    def one_block(inputs_pair):
        block_tokens, block_positions = inputs_pair
        stream = block_tokens.astype(jnp.float32)
        mean_square = lax.optimization_barrier(jnp.mean(stream * stream, axis=1, keepdims=True))
        normed = (stream * lax.rsqrt(mean_square + EPS) * gain_pre.astype(jnp.float32)).astype(jnp.bfloat16)
        projected = jnp.dot(normed, qkv_weight, preferred_element_type=jnp.float32)
        head_out = attend(projected, block_positions)
        summed = jnp.zeros((block_tokens.shape[0], D), jnp.float32)
        for member in range(N_TP):
            partial_sum = jnp.dot(head_out[:, member * row_span:(member + 1) * row_span], out_weight[member * row_span:(member + 1) * row_span], preferred_element_type=jnp.float32).astype(jnp.bfloat16)
            partial_sum = lax.optimization_barrier(partial_sum)
            summed = summed + partial_sum.astype(jnp.float32)
        mean_out = lax.optimization_barrier(jnp.mean(summed * summed, axis=1, keepdims=True))
        return (stream + summed * lax.rsqrt(mean_out + EPS) * gain_post.astype(jnp.float32)).astype(jnp.bfloat16)
    result = lax.map(one_block, (tokens.reshape(N_REP, TOK_DEV, D), positions.reshape(N_REP, TOK_DEV)))
    return result.reshape(TOKENS, D)
```

```python
import math

import jax
import jax.numpy as jnp
import numpy as np
from jax import lax
from jax.experimental import pallas as pl
from jax.experimental.pallas import tpu as pltpu
from jax.sharding import PartitionSpec as P

D = 4608
TOK = 1024
HDIM = 128
CHUNK = 256
N_CHUNK = TOK // CHUNK
SEG = 576
PART = 144
QUERY_SCALE = 1.0 / 12.0
EPS = 1e-06
MESH = pl.DeviceIdType.MESH
F32 = jnp.float32
BF16 = jnp.bfloat16
NT = (((1,), (1,)), ((), ()))
W_ROWS = ((0, 192), (192, 192), (384, 192))
W_ORDER = ("xzy", "yzx", "xyz")


def device(x, y, z, c):
    return ((z % 2) * 8 + y * 2 + c, (z // 2) * 4 + x)


def kernel(
    tok, gpre, gpost, freq, qkv, outs, smap, pos, o_hbm,
    s1, send2, wq, w, h0, h1, h2, h3, normed, qb, kb, vb, cosb, sinb, startb, lhs, att, stream, result,
    s1_ss, s1_rs, s2_ss, s2_rs, s3_ss, s3_rs, w_ss, w_rs, h_ss, h_rs, loc,
):
    hs = (h0, h1, h2, h3)
    rep = lax.axis_index("rep")
    tp = lax.axis_index("tp")
    c, y, zl = rep % 2, (rep // 2) % 4, rep // 8
    x, zh = tp % 4, tp // 4
    z = zh * 2 + zl
    yp, ym, y2 = (y + 1) % 4, (y + 3) % 4, (y + 2) % 4

    def shifted(axis, by):
        at = {"x": x, "y": y, "z": z}
        at[axis] = (at[axis] + by + 4) % 4
        return device(at["x"], at["y"], at["z"], c)

    def remote(src, dst, ss, rs, dev):
        return pltpu.make_async_remote_copy(
            src_ref=src, dst_ref=dst, send_sem=ss, recv_sem=rs, device_id=dev, device_id_type=MESH
        )

    tok_copies = []
    for i in range(N_CHUNK):
        rows = pl.ds(i * CHUNK, CHUNK)
        cp = pltpu.make_async_copy(tok.at[rows], normed.at[rows], loc.at[i])
        cp.start()
        tok_copies.append(cp)

    barrier = pltpu.get_barrier_semaphore()

    def greet_rep(d, _):
        pl.semaphore_signal(barrier, inc=1, device_id=((rep + d) % 16, tp), device_id_type=MESH)
        return 0

    def greet_tp(d, _):
        pl.semaphore_signal(barrier, inc=1, device_id=(rep, (tp + d) % 8), device_id_type=MESH)
        return 0

    lax.fori_loop(1, 16, greet_rep, 0)
    lax.fori_loop(1, 8, greet_tp, 0)
    far = jnp.where(zl == 0, 3, 1)
    pl.semaphore_signal(barrier, inc=1, device_id=device(x, y, (z + far) % 4, c), device_id_type=MESH)
    pl.semaphore_wait(barrier, 23)

    def s1_src(to):
        rows = pl.ds(pl.multiple_of(((to // 2) % 4) * PART, 16), PART)
        cols = pl.ds(pl.multiple_of((to // 8) * 128, 128), 128)
        return qkv.at[0, rows, cols]

    own1 = pltpu.make_async_copy(s1_src(rep), s1.at[rep], loc.at[4])
    own1.start()

    def s1_copy(d):
        to = (rep + d) % 16
        return remote(s1_src(to), s1.at[rep], s1_ss.at[d], s1_rs.at[d], (to, tp))

    def s1_start(d, _):
        s1_copy(d).start()
        return 0

    lax.fori_loop(1, 16, s1_start, 0)

    eye = (
        lax.broadcasted_iota(jnp.int32, (SEG, SEG), 0) == lax.broadcasted_iota(jnp.int32, (SEG, SEG), 1)
    ).astype(BF16)
    w[z, y, c, x] = lax.dot_general(eye, outs[0], NT, preferred_element_type=F32).astype(BF16)

    def w_set(part, step):
        r0, n = W_ROWS[part]
        done = W_ORDER[part][:step]
        at = {"x": x, "y": y, "z": z}
        full = slice(None)
        return w.at[
            full if "z" in done else at["z"],
            full if "y" in done else at["y"],
            c,
            full if "x" in done else at["x"],
            pl.ds(r0, n),
        ]

    w_by = (1, -1, 2)

    def w_copies(part, step):
        axis = W_ORDER[part][step]
        block = w_set(part, step)
        return [
            remote(block, block, w_ss.at[part, step, k], w_rs.at[part, step, k], shifted(axis, by))
            for k, by in enumerate(w_by)
        ]

    def w_start(step):
        for part in range(3):
            for cp in w_copies(part, step):
                cp.start()

    def w_wait(step):
        for part in range(3):
            for cp in w_copies(part, step):
                cp.wait_recv()

    w_start(0)

    lax.fori_loop(1, 16, lambda d, _: (s1_copy(d).wait_recv(), 0)[1], 0)
    own1.wait()

    def order_of(b):
        at = jnp.int32(0)
        for s in range(16):
            at = jnp.where(smap[s] == b, s, at)
        return at

    for t in range(8):
        send2[t] = s1[order_of(2 * t + c)]
    g = c * 2 + zl
    g2 = c * 2 + (1 - zl)

    own2 = pltpu.make_async_copy(send2.at[tp], wq.at[g, tp, y], loc.at[5])
    own2.start()

    def s2_copy(d):
        to = (tp + d) % 8
        return remote(send2.at[to], wq.at[g, tp, y], s2_ss.at[d], s2_rs.at[d], (rep, to))

    lax.fori_loop(1, 8, lambda d, _: (s2_copy(d).start(), 0)[1], 0)

    gain = gpre[...]

    def norm_rows(i, _):
        rows = pl.ds(pl.multiple_of(i * 32, 32), 32)
        v = normed[rows, :].astype(F32)
        ms = jnp.sum(v * v, axis=1, keepdims=True) * (1.0 / D)
        normed[rows, :] = (v * lax.rsqrt(ms + EPS) * gain).astype(BF16)
        return 0

    for cp in tok_copies:
        cp.wait()
    lax.fori_loop(0, TOK // 32, norm_rows, 0)

    w_wait(0)
    w_start(1)

    lax.fori_loop(1, 8, lambda d, _: (s2_copy(d).wait_recv(), 0)[1], 0)
    own2.wait()

    zdev = (((1 - zl) * 8 + y * 2 + c), tp)
    sib = (rep + 1 - 2 * c, tp)
    updev, dndev = shifted("y", 1), shifted("y", -1)
    lo, hi = pl.ds(0, 4), pl.ds(4, 4)
    k3 = [0]
    s3 = []

    def s3_send(block, dev):
        k = k3[0]
        k3[0] += 1
        cp = remote(block, block, s3_ss.at[k], s3_rs.at[k], dev)
        cp.start()
        s3.append(cp)
        return cp

    mine, theirs = wq.at[g, :, y], wq.at[g2, :, y]
    z_cp = s3_send(mine, zdev)
    up_a = s3_send(mine, updev)
    dn_a = s3_send(mine, dndev)
    sibs = [s3_send(mine, sib)]
    pos_t = pos[...].astype(F32).T
    lane = lax.broadcasted_iota(jnp.int32, (128, 128), 1)
    for i in range(8):
        p = pos_t[:, i:i + 1]
        angle = p * freq[...]
        rows = pl.ds(i * 128, 128)
        cosb[rows, :] = jnp.cos(angle)
        sinb[rows, :] = jnp.where(lane < 64, -1.0, 1.0) * jnp.sin(angle)
        row = (lax.broadcasted_iota(jnp.int32, (128, 128), 0) + i * 128)
        startb[rows, :] = row - p.astype(jnp.int32)
    z_cp.wait_recv()
    up_b = s3_send(theirs, updev)
    dn_b = s3_send(theirs, dndev)
    sibs.append(s3_send(theirs, sib))
    up_a.wait_recv()
    f1 = s3_send(wq.at[g, lo, ym], updev)
    sibs.append(s3_send(wq.at[g, :, ym], sib))
    dn_a.wait_recv()
    f2 = s3_send(wq.at[g, hi, yp], dndev)
    sibs.append(s3_send(wq.at[g, :, yp], sib))
    w_wait(1)
    w_start(2)
    up_b.wait_recv()
    f3 = s3_send(wq.at[g2, lo, ym], updev)
    sibs.append(s3_send(wq.at[g2, :, ym], sib))
    dn_b.wait_recv()
    f4 = s3_send(wq.at[g2, hi, yp], dndev)
    sibs.append(s3_send(wq.at[g2, :, yp], sib))
    for f, block in (
        (f1, wq.at[g, lo, y2]), (f2, wq.at[g, hi, y2]), (f3, wq.at[g2, lo, y2]), (f4, wq.at[g2, hi, y2])
    ):
        f.wait_recv()
        sibs.append(s3_send(block, sib))
    for cp in sibs:
        cp.wait_recv()

    def project(i):
        rows = pl.ds(i * CHUNK, CHUNK)
        weights = jnp.concatenate([wq[j].reshape(D, 128) for j in range(4)], axis=1)
        p = jnp.dot(normed[rows, :], weights, preferred_element_type=F32)
        cos, sin = cosb[rows, :], sinb[rows, :]

        def rotate(u):
            return u * cos + pltpu.roll(u, 64, 1) * sin

        for j in range(2):
            qb[j, rows, :] = (rotate(p[:, j * 128:(j + 1) * 128]) * QUERY_SCALE).astype(BF16)
        kb[rows, :] = rotate(p[:, 256:384]).astype(BF16)
        vb[rows, :] = p[:, 384:].astype(BF16)

    def attend(i):
        rows = pl.ds(i * CHUNK, CHUNK)
        n = (i + 1) * CHUNK
        first = startb[rows, 0:1]
        at = lax.broadcasted_iota(jnp.int32, (CHUNK, n), 1)
        row = lax.broadcasted_iota(jnp.int32, (CHUNK, n), 0) + i * CHUNK
        allowed = (at <= row) & (at >= first)
        for j in range(2):
            s = lax.dot_general(qb[j, rows, :], kb[0:n, :], NT, preferred_element_type=F32)
            s = jnp.where(allowed, s, -1e30)
            e = jnp.exp(s - jnp.max(s, axis=1, keepdims=True))
            a = (e * (1.0 / jnp.sum(e, axis=1, keepdims=True))).astype(BF16)
            hs[i][zh, x, j] = jnp.dot(a, vb[0:n, :], preferred_element_type=F32).astype(BF16)

    def h_copy(i, d):
        to = (tp + d) % 8
        block = hs[i].at[zh, x]
        return remote(block, block, h_ss.at[i, d], h_rs.at[i, d], (rep, to))

    for i in range(N_CHUNK):
        project(i)
        attend(i)
        lax.fori_loop(1, 8, lambda d, _: (h_copy(i, d).start(), 0)[1], 0)

    w_wait(2)
    w_sib = []
    for part in range(3):
        r0, n = W_ROWS[part]
        for k in range(2):
            block = w.at[pl.ds(2 * k, 2), :, c, :, pl.ds(r0, n)]
            cp = remote(block, block, w_ss.at[part, 3, k], w_rs.at[part, 3, k], sib)
            cp.start()
            w_sib.append(cp)
    for cp in w_sib:
        cp.wait_recv()

    def out_proj(i):
        rows = pl.ds(i * CHUNK, CHUNK)
        st = pltpu.make_async_copy(tok.at[rows], stream.at[i % 2], loc.at[6 + i % 2])
        st.start()
        for s in range(16):
            b = smap[s]
            lhs[:, s * 128:(s + 1) * 128] = hs[i][b // 8, (b // 2) % 4, b % 2]
        left = lhs[...]
        total = jnp.zeros((CHUNK, 1), F32)
        for half in range(2):
            for k in range(3):
                pieces = []
                n = k * 768
                while n < (k + 1) * 768:
                    xi, r0 = n // SEG, n % SEG
                    r1 = min(SEG, r0 + (k + 1) * 768 - n)
                    pieces.append((xi, r0, r1))
                    n += r1 - r0
                right = jnp.concatenate(
                    [
                        jnp.concatenate(
                            [w[half * 2 + r // 8, (r // 2) % 4, r % 2, xi, r0:r1, :] for xi, r0, r1 in pieces], axis=0
                        )
                        for r in range(16)
                    ],
                    axis=1,
                )
                t = lax.dot_general(left, right, NT, preferred_element_type=F32)
                total = total + jnp.sum(t * t, axis=1, keepdims=True)
                col = half * 2304 + k * 768
                att[:, col:col + 768] = t
        scale = lax.rsqrt(total * (1.0 / D) + EPS)
        st.wait()
        if i >= 2:
            pltpu.make_async_copy(
                result.at[i % 2], o_hbm.at[pl.ds((i - 2) * CHUNK, CHUNK)], loc.at[8 + i % 2]
            ).wait()
        att_scale = scale
        result[i % 2] = (stream[i % 2].astype(F32) + att[...] * att_scale * gpost[...]).astype(BF16)
        pltpu.make_async_copy(result.at[i % 2], o_hbm.at[rows], loc.at[8 + i % 2]).start()

    for i in range(N_CHUNK):
        lax.fori_loop(1, 8, lambda d, _: (h_copy(i, d).wait_recv(), 0)[1], 0)
        out_proj(i)

    lax.fori_loop(1, 16, lambda d, _: (s1_copy(d).wait_send(), 0)[1], 0)
    lax.fori_loop(1, 8, lambda d, _: (s2_copy(d).wait_send(), 0)[1], 0)
    for cp in s3:
        cp.wait_send()
    for step in range(3):
        for part in range(3):
            for cp in w_copies(part, step):
                cp.wait_send()
    for cp in w_sib:
        cp.wait_send()
    for i in range(N_CHUNK):
        lax.fori_loop(1, 8, lambda d, _: (h_copy(i, d).wait_send(), 0)[1], 0)
    for i in (2, 3):
        pltpu.make_async_copy(result.at[i % 2], o_hbm.at[pl.ds(i * CHUNK, CHUNK)], loc.at[8 + i % 2]).wait()


def on_device(tokens, gain_pre, gain_post, qkv_shards, out_shards, shard_map, positions):
    freq = np.exp(np.arange(64) * (-2.0 * math.log(10000.0) / HDIM)).astype(np.float32)
    freq = jnp.asarray(np.concatenate([freq, freq])[None])
    vmem, hbm = pl.BlockSpec(memory_space=pltpu.VMEM), pl.BlockSpec(memory_space=pl.ANY)
    smem = pl.BlockSpec(memory_space=pltpu.SMEM)
    sem = pltpu.SemaphoreType.DMA
    heads = pltpu.VMEM((2, 4, 2, CHUNK, 128), BF16)
    return pl.pallas_call(
        kernel,
        name="attention_block",
        out_shape=jax.ShapeDtypeStruct((TOK, D), BF16),
        in_specs=[hbm, vmem, vmem, vmem, hbm, vmem, smem, vmem],
        out_specs=hbm,
        scratch_shapes=[
            pltpu.VMEM((16, PART, 128), BF16),
            pltpu.VMEM((8, PART, 128), BF16),
            pltpu.VMEM((4, 8, 4, PART, 128), BF16),
            pltpu.VMEM((4, 4, 2, 4, SEG, 128), BF16),
            heads, heads, heads, heads,
            pltpu.VMEM((TOK, D), BF16),
            pltpu.VMEM((2, TOK, 128), BF16),
            pltpu.VMEM((TOK, 128), BF16),
            pltpu.VMEM((TOK, 128), BF16),
            pltpu.VMEM((TOK, 128), F32),
            pltpu.VMEM((TOK, 128), F32),
            pltpu.VMEM((TOK, 128), jnp.int32),
            pltpu.VMEM((CHUNK, 2048), BF16),
            pltpu.VMEM((CHUNK, D), F32),
            pltpu.VMEM((2, CHUNK, D), BF16),
            pltpu.VMEM((2, CHUNK, D), BF16),
            sem((16,)), sem((16,)), sem((8,)), sem((8,)), sem((24,)), sem((24,)),
            sem((3, 4, 3)), sem((3, 4, 3)), sem((4, 8)), sem((4, 8)), sem((10,)),
        ],
        compiler_params=pltpu.CompilerParams(
            collective_id=0, has_side_effects=True, vmem_limit_bytes=62 << 20
        ),
        cost_estimate=pl.CostEstimate(flops=26 * 10**9, bytes_accessed=30 * 10**6, transcendentals=3 * 10**6),
    )(
        tokens, gain_pre.reshape(1, D), gain_post.reshape(1, D), freq, qkv_shards, out_shards, shard_map,
        positions.reshape(8, 128),
    )


def solution(mesh):
    placed = (P("rep", None), P(), P(), P("rep", "tp", None), P("rep", None, "tp"), P(), P("rep"))
    return jax.shard_map(
        on_device, mesh=mesh, in_specs=placed, out_specs=P("rep", None), check_vma=False
    )
```

```python
import math

import jax
import jax.numpy as jnp
import numpy as np
from jax import lax
from jax.experimental import pallas as pl
from jax.experimental.pallas import tpu as pltpu
from jax.sharding import PartitionSpec as P

D = 4608
TOK = 1024
HDIM = 128
CHUNK = 256
N_CHUNK = TOK // CHUNK
SEG = 576
PART = 144
QUERY_SCALE = 1.0 / 12.0
EPS = 1e-06
MESH = pl.DeviceIdType.MESH
F32 = jnp.float32
BF16 = jnp.bfloat16
NT = (((1,), (1,)), ((), ()))
W_N = (256, 192, 128)
W_OFF = ((0, 320), (384, 0), (256, 192))
W_ORDER = ("yzx", "xyz", "zxy")
W_COL = ((0, 896), (384, 576), (256, 768))


def device(x, y, z, c):
    return ((z % 2) * 8 + y * 2 + c, (z // 2) * 4 + x)


def kernel(
    tok, gpre, gpost, freq, qkv, outs, smap, pos, o_ref,
    s1, send2, wq, wa, wb, wc, h0, h1, h2, h3, normed, qb, kv, cosb, sinb, startb, total, gain1, gain2,
    s1_ss, s1_rs, s2_ss, s2_rs, s3_ss, s3_rs, w_ss, w_rs, h_ss, h_rs, loc,
):
    hs = (h0, h1, h2, h3)
    ws = (wa, wb, wc)
    rep = lax.axis_index("rep")
    tp = lax.axis_index("tp")
    c, y, zl = rep % 2, (rep // 2) % 4, rep // 8
    x, zh = tp % 4, tp // 4
    z = zh * 2 + zl
    yp, ym, y2 = (y + 1) % 4, (y + 3) % 4, (y + 2) % 4
    xp, xm, x2 = (x + 1) % 4, (x + 3) % 4, (x + 2) % 4
    full = slice(None)

    def shifted(axis, by):
        at = {"x": x, "y": y, "z": z}
        at[axis] = (at[axis] + by + 4) % 4
        return device(at["x"], at["y"], at["z"], c)

    def remote(src, dst, ss, rs, dev):
        return pltpu.make_async_remote_copy(
            src_ref=src, dst_ref=dst, send_sem=ss, recv_sem=rs, device_id=dev, device_id_type=MESH
        )

    started = []

    def go(cp):
        cp.start()
        started.append(cp)
        return cp

    tok_copies = []
    for i in range(N_CHUNK):
        rows = pl.ds(i * CHUNK, CHUNK)
        cp = pltpu.make_async_copy(tok.at[rows], o_ref.at[rows], loc.at[i])
        cp.start()
        tok_copies.append(cp)
    w_own = []
    for p in range(3):
        off = pl.multiple_of(jnp.where(x % 2 == 0, W_OFF[p][0], W_OFF[p][1]), 64)
        cp = pltpu.make_async_copy(outs.at[0, pl.ds(off, W_N[p])], ws[p].at[z, y, c, x], loc.at[6 + p])
        cp.start()
        w_own.append(cp)

    barrier = pltpu.get_barrier_semaphore()

    def greet_rep(d, _):
        pl.semaphore_signal(barrier, inc=1, device_id=((rep + d) % 16, tp), device_id_type=MESH)
        return 0

    def greet_tp(d, _):
        pl.semaphore_signal(barrier, inc=1, device_id=(rep, (tp + d) % 8), device_id_type=MESH)
        return 0

    lax.fori_loop(1, 16, greet_rep, 0)
    lax.fori_loop(1, 8, greet_tp, 0)
    far = jnp.where(zl == 0, 3, 1)
    pl.semaphore_signal(barrier, inc=1, device_id=device(x, y, (z + far) % 4, c), device_id_type=MESH)
    pl.semaphore_wait(barrier, 23)

    place = rep // 2
    sib = (rep + 1 - 2 * c, tp)

    def s1_src(to):
        rows = pl.ds(pl.multiple_of((to % 4) * PART, 16), PART)
        cols = pl.ds(pl.multiple_of((to // 4) * 128, 128), 128)
        return qkv.at[0, rows, cols]

    own1 = pltpu.make_async_copy(s1_src(place), s1.at[place, c], loc.at[4])
    own1.start()

    def s1_copy(d):
        to = (place + d) % 8
        return remote(s1_src(to), s1.at[place, c], s1_ss.at[d], s1_rs.at[d], (to * 2 + c, tp))

    lax.fori_loop(1, 8, lambda d, _: (s1_copy(d).start(), 0)[1], 0)

    def w_set(p, done, axis=None, by=0, half=None):
        at = {"x": x, "y": y, "z": z}
        if axis is not None:
            at[axis] = (at[axis] + by + 4) % 4
        n = W_N[p]
        rows = pl.ds(0, n) if half is None else pl.ds(half * (n // 2), n // 2)
        iz, iy, ix = (full if a in done else at[a] for a in "zyx")
        return ws[p].at[iz, iy, c, ix, rows]

    w_in = {}

    def w_send(p, step):
        axis, done = W_ORDER[p][step], W_ORDER[p][:step]
        ways = ((1, 0), (-1, 1), (1, 1), (-1, 0)) if step == 2 else ((1, None), (-1, None), (2, None))
        cps = []
        for k, (by, half) in enumerate(ways):
            block = w_set(p, done, half=half)
            cps.append(go(remote(block, block, w_ss.at[p, step, k], w_rs.at[p, step, k], shifted(axis, by))))
        w_in[p, step] = cps

    def w_wait(p, step):
        for cp in w_in[p, step]:
            cp.wait_recv()

    def w_relay(p):
        axis, done = W_ORDER[p][2], W_ORDER[p][:2]
        cps = w_in[p, 2]
        for k, (by, half) in enumerate(((1, 0), (-1, 1))):
            cps[k].wait_recv()
            block = w_set(p, done, axis, -by, half)
            cps.append(go(remote(block, block, w_ss.at[p, 2, 4 + k], w_rs.at[p, 2, 4 + k], shifted(axis, by))))

    w_sib = {0: [], 1: [], 2: []}

    def w_share(p, by):
        axis, done = W_ORDER[p][2], W_ORDER[p][:2]
        k = len(w_sib[p])
        block = w_set(p, done, axis, by)
        w_sib[p].append(go(remote(block, block, w_ss.at[p, 3, k], w_rs.at[p, 3, k], sib)))

    def w_all(p):
        cps = w_in[p, 2]
        for cp in cps[2:4]:
            cp.wait_recv()
        w_share(p, 1)
        w_share(p, -1)
        for cp in cps[4:]:
            cp.wait_recv()
        w_share(p, 2)

    def w_ready(p):
        for cp in w_sib[p]:
            cp.wait_recv()

    for cp in w_own:
        cp.wait()
    for p in range(3):
        w_send(p, 0)

    for k in range(D // 128):
        gain1[:, k * 128:(k + 1) * 128] = gpre[k:k + 1, :]
        gain2[:, k * 128:(k + 1) * 128] = gpost[k:k + 1, :]

    def norm_rows(i, _):
        rows = pl.ds(pl.multiple_of(i * 32, 32), 32)
        v = o_ref[rows, :].astype(F32)
        ms = jnp.sum(v * v, axis=1, keepdims=True) * (1.0 / D)
        normed[rows, :] = (v * lax.rsqrt(ms + EPS) * gain1[...]).astype(BF16)
        return 0

    for cp in tok_copies:
        cp.wait()
    lax.fori_loop(0, 12, norm_rows, 0)
    for p in range(3):
        w_wait(p, 0)
    for p in range(3):
        w_send(p, 1)
    lax.fori_loop(1, 8, lambda d, _: (s1_copy(d).wait_recv(), 0)[1], 0)
    own1.wait()
    swap = go(remote(s1.at[:, c], s1.at[:, c], s1_ss.at[0], s1_rs.at[0], sib))
    lax.fori_loop(12, 20, norm_rows, 0)
    swap.wait_recv()

    def order_of(b):
        at = jnp.int32(0)
        for s in range(16):
            at = jnp.where(smap[s] == b, s, at)
        return at

    for t in range(8):
        at = order_of(2 * t + c)
        send2[t] = s1[at // 2, at % 2]
    g = c * 2 + zl
    g2 = c * 2 + (1 - zl)

    own2 = pltpu.make_async_copy(send2.at[tp], wq.at[g, tp, y], loc.at[5])
    own2.start()

    def s2_copy(d):
        to = (tp + d) % 8
        return remote(send2.at[to], wq.at[g, tp, y], s2_ss.at[d], s2_rs.at[d], (rep, to))

    lax.fori_loop(1, 8, lambda d, _: (s2_copy(d).start(), 0)[1], 0)
    lax.fori_loop(20, 32, norm_rows, 0)

    lax.fori_loop(1, 8, lambda d, _: (s2_copy(d).wait_recv(), 0)[1], 0)
    own2.wait()

    zdev = ((1 - zl) * 8 + y * 2 + c, tp)
    updev, dndev = shifted("y", 1), shifted("y", -1)
    lo, hi = pl.ds(0, 4), pl.ds(4, 4)
    k3 = [0]

    def s3_send(block, dev):
        k = k3[0]
        k3[0] += 1
        return go(remote(block, block, s3_ss.at[k], s3_rs.at[k], dev))

    z_lo = s3_send(wq.at[g, lo, y], zdev)
    up_lo = s3_send(wq.at[g, lo, y], updev)
    dn_hi = s3_send(wq.at[g, hi, y], dndev)
    z_hi = s3_send(wq.at[g, hi, y], zdev)
    up_hi = s3_send(wq.at[g, hi, y], updev)
    dn_lo = s3_send(wq.at[g, lo, y], dndev)
    sib_a = [s3_send(wq.at[g, :, y], sib)]
    sib_b = []
    for p in range(2):
        w_wait(p, 1)
        w_send(p, 2)
        w_share(p, 0)
    pos_t = pos[...].astype(F32).T
    lane = lax.broadcasted_iota(jnp.int32, (128, 128), 1)
    for i in range(8):
        at = pos_t[:, i:i + 1]
        angle = at * freq[...]
        rows = pl.ds(i * 128, 128)
        cosb[rows, :] = jnp.cos(angle)
        sinb[rows, :] = jnp.where(lane < 64, -1.0, 1.0) * jnp.sin(angle)
        row = lax.broadcasted_iota(jnp.int32, (128, 128), 0) + i * 128
        startb[rows, :] = row - at.astype(jnp.int32)
    up_lo.wait_recv()
    r_up = s3_send(wq.at[g, lo, ym], updev)
    dn_hi.wait_recv()
    r_dn = s3_send(wq.at[g, hi, yp], dndev)
    z_lo.wait_recv()
    up_tlo = s3_send(wq.at[g2, lo, y], updev)
    z_hi.wait_recv()
    dn_thi = s3_send(wq.at[g2, hi, y], dndev)
    up_thi = s3_send(wq.at[g2, hi, y], updev)
    dn_tlo = s3_send(wq.at[g2, lo, y], dndev)
    sib_b.append(s3_send(wq.at[g2, :, y], sib))
    up_hi.wait_recv()
    sib_a.append(s3_send(wq.at[g, :, ym], sib))
    dn_lo.wait_recv()
    sib_a.append(s3_send(wq.at[g, :, yp], sib))
    w_relay(0)
    r_up.wait_recv()
    r_dn.wait_recv()
    sib_a.append(s3_send(wq.at[g, :, y2], sib))
    up_tlo.wait_recv()
    r_tup = s3_send(wq.at[g2, lo, ym], updev)
    dn_thi.wait_recv()
    r_tdn = s3_send(wq.at[g2, hi, yp], dndev)
    w_relay(1)
    w_wait(2, 1)
    w_send(2, 2)
    w_share(2, 0)
    for cp in sib_a:
        cp.wait_recv()

    def project(i, which):
        rows = pl.ds(i * CHUNK, CHUNK)
        weights = jnp.concatenate([wq[which].reshape(D, 128), wq[2 + which].reshape(D, 128)], axis=1)
        p = jnp.dot(normed[rows, :], weights, preferred_element_type=F32)
        cos, sin = cosb[rows, :], sinb[rows, :]

        def rotate(u):
            return u * cos + pltpu.roll(u, 64, 1) * sin

        qb[which, rows, :] = (rotate(p[:, :128]) * QUERY_SCALE).astype(BF16)
        u = p[:, 128:]
        kv[which, rows, :] = jnp.where(which == 0, rotate(u), u).astype(BF16)

    project(0, zl)
    up_thi.wait_recv()
    sib_b.append(s3_send(wq.at[g2, :, ym], sib))
    dn_tlo.wait_recv()
    sib_b.append(s3_send(wq.at[g2, :, yp], sib))
    project(1, zl)
    project(2, zl)
    project(3, zl)
    r_tup.wait_recv()
    r_tdn.wait_recv()
    sib_b.append(s3_send(wq.at[g2, :, y2], sib))
    for cp in sib_b:
        cp.wait_recv()

    def attend(i):
        rows = pl.ds(i * CHUNK, CHUNK)
        n = (i + 1) * CHUNK
        first = startb[rows, 0:1]
        at = lax.broadcasted_iota(jnp.int32, (CHUNK, n), 1)
        row = lax.broadcasted_iota(jnp.int32, (CHUNK, n), 0) + i * CHUNK
        allowed = (at <= row) & (at >= first)
        for j in range(2):
            s = lax.dot_general(qb[j, rows, :], kv[0, 0:n, :], NT, preferred_element_type=F32)
            s = jnp.where(allowed, s, -1e30)
            e = jnp.exp(s - jnp.max(s, axis=1, keepdims=True))
            a = (e * (1.0 / jnp.sum(e, axis=1, keepdims=True))).astype(BF16)
            hs[i][zh, x, j] = jnp.dot(a, kv[1, 0:n, :], preferred_element_type=F32).astype(BF16)

    zpair = (rep, (tp + 4) % 8)
    xup, xdn = shifted("x", 1), shifted("x", -1)
    oz = 1 - zh
    top, bot = pl.ds(0, CHUNK // 2), pl.ds(CHUNK // 2, CHUNK // 2)
    h_in = [dict() for _ in range(N_CHUNK)]

    def h_send(i, name, block, dev):
        k = len(h_in[i])
        h_in[i][name] = go(remote(block, block, h_ss.at[i, k], h_rs.at[i, k], dev))

    def h_got(i, name):
        h_in[i][name].wait_recv()

    def h_stage(i, stage):
        h = hs[i]
        if stage == 0:
            h_send(i, "z0", h.at[zh, x, 0], zpair)
            h_send(i, "u1t", h.at[zh, x, 1, top], xup)
            h_send(i, "d1b", h.at[zh, x, 1, bot], xdn)
            h_send(i, "u1b", h.at[zh, x, 1, bot], xup)
            h_send(i, "d1t", h.at[zh, x, 1, top], xdn)
            h_send(i, "u0t", h.at[zh, x, 0, top], xup)
            h_send(i, "d0b", h.at[zh, x, 0, bot], xdn)
            h_send(i, "u0b", h.at[zh, x, 0, bot], xup)
            h_send(i, "d0t", h.at[zh, x, 0, top], xdn)
            h_send(i, "z1", h.at[zh, x, 1], zpair)
        elif stage == 1:
            h_got(i, "u1t")
            h_send(i, "ru1", h.at[zh, xm, 1, top], xup)
            h_got(i, "d1b")
            h_send(i, "rd1", h.at[zh, xp, 1, bot], xdn)
            h_got(i, "z0")
            h_send(i, "v0t", h.at[oz, x, 0, top], xup)
            h_send(i, "e0b", h.at[oz, x, 0, bot], xdn)
            h_send(i, "v0b", h.at[oz, x, 0, bot], xup)
            h_send(i, "e0t", h.at[oz, x, 0, top], xdn)
            h_got(i, "u1b")
            h_send(i, "zm", h.at[zh, xm, 1], zpair)
            h_got(i, "d1t")
            h_send(i, "zp", h.at[zh, xp, 1], zpair)
        elif stage == 2:
            h_got(i, "u0t")
            h_send(i, "ru0", h.at[zh, xm, 0, top], xup)
            h_got(i, "d0b")
            h_send(i, "rd0", h.at[zh, xp, 0, bot], xdn)
            h_got(i, "ru1")
            h_got(i, "rd1")
            h_send(i, "z2", h.at[zh, x2, 1], zpair)
            h_got(i, "v0t")
            h_send(i, "rv0", h.at[oz, xm, 0, top], xup)
            h_got(i, "e0b")
            h_send(i, "re0", h.at[oz, xp, 0, bot], xdn)
        else:
            for name in ("u0b", "d0t", "v0b", "e0t", "z1", "zm", "zp", "z2", "ru0", "rd0", "rv0", "re0"):
                h_got(i, name)

    def heads_of(i):
        project(i, 1 - zl)
        attend(i)
        h_stage(i, 0)

    heads_of(0)
    heads_of(1)
    w_relay(2)
    h_stage(0, 1)
    heads_of(2)
    w_all(0)
    h_stage(0, 2)
    h_stage(1, 1)
    project(3, 1 - zl)
    attend(3)
    w_all(1)
    h_stage(0, 3)
    h_stage(1, 2)
    h_stage(2, 1)
    h_stage(3, 0)

    def out_proj(p, i):
        rows = pl.ds(i * CHUNK, CHUNK)
        n = W_N[p]
        left = []
        for s in range(16):
            b = smap[s]
            left.append(hs[i][b // 8, (b // 2) % 4, b % 2])
        left = jnp.concatenate(left, axis=1)
        squares = jnp.zeros((CHUNK, 1), F32)
        for half in range(2):
            right = jnp.concatenate(
                [ws[p][half * 2 + r // 8, (r // 2) % 4, r % 2].reshape(4 * n, 128) for r in range(16)], axis=1
            )
            t = lax.dot_general(left, right, NT, preferred_element_type=F32)
            squares = squares + jnp.sum(t * t, axis=1, keepdims=True)
            t = t.astype(BF16)
            for pair in range(2):
                col = half * 2304 + pair * 1152
                a, b = t[:, 2 * pair * n:(2 * pair + 1) * n], t[:, (2 * pair + 1) * n:(2 * pair + 2) * n]
                if p == 1:
                    normed[rows, col + 384:col + 768] = t[:, 2 * pair * n:(2 * pair + 2) * n]
                else:
                    normed[rows, col + W_COL[p][0]:col + W_COL[p][0] + n] = a
                    normed[rows, col + W_COL[p][1]:col + W_COL[p][1] + n] = b
        squares = jnp.broadcast_to(squares, (CHUNK, 128))
        total[rows, :] = squares if p == 0 else total[rows, :] + squares

    def finish(i):
        rows = pl.ds(i * CHUNK, CHUNK)
        scale = lax.rsqrt(total[rows, 0:1] * (1.0 / D) + EPS)
        o_ref[rows, :] = (
            o_ref[rows, :].astype(F32) + normed[rows, :].astype(F32) * scale * gain2[...]
        ).astype(BF16)

    w_ready(0)
    out_proj(0, 0)
    h_stage(1, 3)
    h_stage(2, 2)
    w_ready(1)
    out_proj(1, 0)
    h_stage(3, 1)
    out_proj(0, 1)
    out_proj(1, 1)
    w_all(2)
    h_stage(2, 3)
    w_ready(2)
    out_proj(2, 0)
    finish(0)
    h_stage(3, 2)
    out_proj(2, 1)
    finish(1)
    for p in range(3):
        out_proj(p, 2)
    finish(2)
    h_stage(3, 3)
    for p in range(3):
        out_proj(p, 3)
    finish(3)

    lax.fori_loop(1, 8, lambda d, _: (s1_copy(d).wait_send(), 0)[1], 0)
    lax.fori_loop(1, 8, lambda d, _: (s2_copy(d).wait_send(), 0)[1], 0)
    for cp in started:
        cp.wait_send()


def on_device(tokens, gain_pre, gain_post, qkv_shards, out_shards, shard_map, positions):
    freq = np.exp(np.arange(64) * (-2.0 * math.log(10000.0) / HDIM)).astype(np.float32)
    freq = jnp.asarray(np.concatenate([freq, freq])[None])
    vmem, hbm = pl.BlockSpec(memory_space=pltpu.VMEM), pl.BlockSpec(memory_space=pl.ANY)
    smem = pl.BlockSpec(memory_space=pltpu.SMEM)
    sem = pltpu.SemaphoreType.DMA
    heads = pltpu.VMEM((2, 4, 2, CHUNK, 128), BF16)
    return pl.pallas_call(
        kernel,
        name="attention_block",
        out_shape=pltpu.VMEM((TOK, D), BF16),
        in_specs=[hbm, vmem, vmem, vmem, hbm, hbm, smem, vmem],
        out_specs=vmem,
        scratch_shapes=[
            pltpu.VMEM((8, 2, PART, 128), BF16),
            pltpu.VMEM((8, PART, 128), BF16),
            pltpu.VMEM((4, 8, 4, PART, 128), BF16),
            *[pltpu.VMEM((4, 4, 2, 4, n, 128), BF16) for n in W_N],
            heads, heads, heads, heads,
            pltpu.VMEM((TOK, D), BF16),
            pltpu.VMEM((2, TOK, 128), BF16),
            pltpu.VMEM((2, TOK, 128), BF16),
            pltpu.VMEM((TOK, 128), F32),
            pltpu.VMEM((TOK, 128), F32),
            pltpu.VMEM((TOK, 128), jnp.int32),
            pltpu.VMEM((TOK, 128), F32),
            pltpu.VMEM((1, D), F32),
            pltpu.VMEM((1, D), F32),
            sem((8,)), sem((8,)), sem((8,)), sem((8,)), sem((32,)), sem((32,)),
            sem((3, 4, 6)), sem((3, 4, 6)), sem((4, 24)), sem((4, 24)), sem((12,)),
        ],
        compiler_params=pltpu.CompilerParams(
            collective_id=0, has_side_effects=True, vmem_limit_bytes=52 << 20
        ),
        cost_estimate=pl.CostEstimate(flops=26 * 10**9, bytes_accessed=30 * 10**6, transcendentals=3 * 10**6),
    )(
        tokens, gain_pre.reshape(D // 128, 128), gain_post.reshape(D // 128, 128), freq, qkv_shards, jnp.swapaxes(out_shards, 1, 2),
        shard_map, positions.reshape(8, 128),
    )


def solution(mesh):
    placed = (P("rep", None), P(), P(), P("rep", "tp", None), P("rep", None, "tp"), P(), P("rep"))
    return jax.shard_map(
        on_device, mesh=mesh, in_specs=placed, out_specs=P("rep", None), check_vma=False
    )
```

```python
import math

import jax
import jax.numpy as jnp
import numpy as np
from jax import lax
from jax.experimental import pallas as pl
from jax.experimental.pallas import tpu as pltpu
from jax.sharding import PartitionSpec as P

D = 4608
TOK = 1024
HDIM = 128
CHUNK = 256
N_CHUNK = TOK // CHUNK
SEG = 576
PART = 144
QUERY_SCALE = 1.0 / 12.0
EPS = 1e-06
MESH = pl.DeviceIdType.MESH
F32 = jnp.float32
BF16 = jnp.bfloat16
NT = (((1,), (1,)), ((), ()))
W_N = (192, 256, 128)
W_OFF = ((384, 0), (0, 320), (256, 192))
W_ORDER = ("zyx", "xzy", "yxz")
W_COL = ((384, 576), (0, 896), (256, 768))


def device(x, y, z, c):
    return ((z % 2) * 8 + y * 2 + c, (z // 2) * 4 + x)


def kernel(
    tok, gpre, gpost, freq, qkv, outs, smap, pos, o_ref,
    s1, send2, wq, wa, wb, wc, h0, h1, h2, h3, normed, qb, kv, cosb, sinb, startb, total, gain1, gain2,
    s1_ss, s1_rs, s2_ss, s2_rs, s3_ss, s3_rs, w_ss, w_rs, v_ss, v_rs, h_ss, h_rs, loc,
):
    hs = (h0, h1, h2, h3)
    ws = (wa, wb, wc)
    rep = lax.axis_index("rep")
    tp = lax.axis_index("tp")
    c, y, zl = rep % 2, (rep // 2) % 4, rep // 8
    x, zh = tp % 4, tp // 4
    z = zh * 2 + zl
    yp, ym, y2 = (y + 1) % 4, (y + 3) % 4, (y + 2) % 4
    xp, xm, x2 = (x + 1) % 4, (x + 3) % 4, (x + 2) % 4
    full = slice(None)

    def shifted(axis, by):
        at = {"x": x, "y": y, "z": z}
        at[axis] = (at[axis] + by + 4) % 4
        return device(at["x"], at["y"], at["z"], c)

    def remote(src, dst, ss, rs, dev):
        return pltpu.make_async_remote_copy(
            src_ref=src, dst_ref=dst, send_sem=ss, recv_sem=rs, device_id=dev, device_id_type=MESH
        )

    started = []

    def go(cp):
        cp.start()
        started.append(cp)
        return cp

    tok_copies = []
    for i in range(N_CHUNK):
        rows = pl.ds(i * CHUNK, CHUNK)
        cp = pltpu.make_async_copy(tok.at[rows], o_ref.at[rows], loc.at[i])
        cp.start()
        tok_copies.append(cp)
    w_own = []
    for p in range(3):
        off = pl.multiple_of(jnp.where(x % 2 == 0, W_OFF[p][0], W_OFF[p][1]), 64)
        cp = pltpu.make_async_copy(outs.at[0, pl.ds(off, W_N[p])], ws[p].at[z, y, c, x], loc.at[6 + p])
        cp.start()
        w_own.append(cp)

    barrier = pltpu.get_barrier_semaphore()

    def greet_rep(d, _):
        pl.semaphore_signal(barrier, inc=1, device_id=((rep + d) % 16, tp), device_id_type=MESH)
        return 0

    def greet_tp(d, _):
        pl.semaphore_signal(barrier, inc=1, device_id=(rep, (tp + d) % 8), device_id_type=MESH)
        return 0

    lax.fori_loop(1, 16, greet_rep, 0)
    lax.fori_loop(1, 8, greet_tp, 0)
    far = jnp.where(zl == 0, 3, 1)
    pl.semaphore_signal(barrier, inc=1, device_id=device(x, y, (z + far) % 4, c), device_id_type=MESH)
    pl.semaphore_wait(barrier, 23)

    place = rep // 2
    sib = (rep + 1 - 2 * c, tp)

    def s1_src(to):
        rows = pl.ds(pl.multiple_of((to % 4) * PART, 16), PART)
        cols = pl.ds(pl.multiple_of((to // 4) * 128, 128), 128)
        return qkv.at[0, rows, cols]

    own1 = pltpu.make_async_copy(s1_src(place), s1.at[place, c], loc.at[4])
    own1.start()

    def s1_copy(d):
        to = (place + d) % 8
        return remote(s1_src(to), s1.at[place, c], s1_ss.at[d], s1_rs.at[d], (to * 2 + c, tp))

    lax.fori_loop(1, 8, lambda d, _: (s1_copy(d).start(), 0)[1], 0)

    def w_set(p, done, axis=None, by=0, half=None):
        at = {"x": x, "y": y, "z": z}
        if axis is not None:
            at[axis] = (at[axis] + by + 4) % 4
        n = W_N[p]
        rows = pl.ds(0, n) if half is None else pl.ds(half * (n // 2), n // 2)
        iz, iy, ix = (full if a in done else at[a] for a in "zyx")
        return ws[p].at[iz, iy, c, ix, rows]

    w_in = {}

    def w_send(p, step):
        axis, done = W_ORDER[p][step], W_ORDER[p][:step]
        cps = []
        for k, by in enumerate((1, -1, 2)):
            block = w_set(p, done)
            cps.append(go(remote(block, block, w_ss.at[p, step, k], w_rs.at[p, step, k], shifted(axis, by))))
        w_in[p, step] = cps

    def w_wait(p, step):
        for cp in w_in[p, step]:
            cp.wait_recv()

    ways = ((1, 0), (-1, 1), (1, 1), (-1, 0))
    v_in = {}

    def v_block(p, q, by, half):
        first, second, last = W_ORDER[p]
        at = {"x": x, "y": y, "z": z}
        at[second] = (at[second] + (0, 1, 3, 2)[q]) % 4
        at[last] = (at[last] + by + 4) % 4
        at[first] = full
        n = W_N[p] // 2
        return ws[p].at[at["z"], at["y"], c, at["x"], pl.ds(half * n, n)]

    def v_send(p, qs):
        for k, (by, half) in enumerate(ways):
            for q in qs:
                block = v_block(p, q, 0, half)
                cp = remote(block, block, v_ss.at[p, q, k], v_rs.at[p, q, k], shifted(W_ORDER[p][2], by))
                v_in[p, q, k] = go(cp)

    def v_relay(p, qs):
        for k in range(2):
            by, half = ways[k]
            for q in qs:
                v_in[p, q, k].wait_recv()
                block = v_block(p, q, -by, half)
                cp = remote(block, block, v_ss.at[p, q, 4 + k], v_rs.at[p, q, 4 + k], shifted(W_ORDER[p][2], by))
                v_in[p, q, 4 + k] = go(cp)

    w_sib = {0: [], 1: [], 2: []}

    def w_share(p, by):
        axis, done = W_ORDER[p][2], W_ORDER[p][:2]
        k = len(w_sib[p])
        block = w_set(p, done, axis, by)
        w_sib[p].append(go(remote(block, block, w_ss.at[p, 3, k], w_rs.at[p, 3, k], sib)))

    def w_near(p):
        for q in range(4):
            v_in[p, q, 2].wait_recv()
            v_in[p, q, 3].wait_recv()
        w_share(p, 1)
        w_share(p, -1)

    def w_far(p):
        for q in range(4):
            v_in[p, q, 4].wait_recv()
            v_in[p, q, 5].wait_recv()
        w_share(p, 2)

    def w_ready(p, first=0, last=4):
        for cp in w_sib[p][first:last]:
            cp.wait_recv()

    for cp in w_own:
        cp.wait()
    for p in range(3):
        w_send(p, 0)

    for k in range(D // 128):
        gain1[:, k * 128:(k + 1) * 128] = gpre[k:k + 1, :]
        gain2[:, k * 128:(k + 1) * 128] = gpost[k:k + 1, :]

    def norm_rows(i, _):
        rows = pl.ds(pl.multiple_of(i * 32, 32), 32)
        v = o_ref[rows, :].astype(F32)
        ms = jnp.sum(v * v, axis=1, keepdims=True) * (1.0 / D)
        normed[rows, :] = (v * lax.rsqrt(ms + EPS) * gain1[...]).astype(BF16)
        return 0

    for cp in tok_copies:
        cp.wait()
    lax.fori_loop(0, 8, norm_rows, 0)
    w_wait(0, 0)
    w_send(0, 1)
    v_send(0, (0,))
    w_wait(2, 0)
    v_send(2, (0,))
    lax.fori_loop(8, 14, norm_rows, 0)
    lax.fori_loop(1, 8, lambda d, _: (s1_copy(d).wait_recv(), 0)[1], 0)
    own1.wait()
    swap = go(remote(s1.at[:, c], s1.at[:, c], s1_ss.at[0], s1_rs.at[0], sib))
    lax.fori_loop(14, 22, norm_rows, 0)
    swap.wait_recv()

    def order_of(b):
        at = jnp.int32(0)
        for s in range(16):
            at = jnp.where(smap[s] == b, s, at)
        return at

    for t in range(8):
        at = order_of(2 * t + c)
        send2[t] = s1[at // 2, at % 2]
    g = c * 2 + zl
    g2 = c * 2 + (1 - zl)

    own2 = pltpu.make_async_copy(send2.at[tp], wq.at[g, tp, y], loc.at[5])
    own2.start()

    def s2_copy(d):
        to = (tp + d) % 8
        return remote(send2.at[to], wq.at[g, tp, y], s2_ss.at[d], s2_rs.at[d], (rep, to))

    lax.fori_loop(1, 8, lambda d, _: (s2_copy(d).start(), 0)[1], 0)
    v_relay(0, (0,))
    w_send(2, 1)
    v_relay(2, (0,))
    w_wait(1, 0)
    lax.fori_loop(22, 32, norm_rows, 0)

    lax.fori_loop(1, 8, lambda d, _: (s2_copy(d).wait_recv(), 0)[1], 0)
    own2.wait()

    zdev = ((1 - zl) * 8 + y * 2 + c, tp)
    updev, dndev = shifted("y", 1), shifted("y", -1)
    lo, hi = pl.ds(0, 4), pl.ds(4, 4)
    k3 = [0]

    def s3_send(block, dev):
        k = k3[0]
        k3[0] += 1
        return go(remote(block, block, s3_ss.at[k], s3_rs.at[k], dev))

    z_lo = s3_send(wq.at[g, lo, y], zdev)
    up_lo = s3_send(wq.at[g, lo, y], updev)
    dn_hi = s3_send(wq.at[g, hi, y], dndev)
    z_hi = s3_send(wq.at[g, hi, y], zdev)
    up_hi = s3_send(wq.at[g, hi, y], updev)
    dn_lo = s3_send(wq.at[g, lo, y], dndev)
    sib_a = [s3_send(wq.at[g, :, y], sib)]
    sib_b = []
    w_send(1, 1)
    w_wait(0, 1)
    v_send(0, (1, 2, 3))
    w_share(0, 0)
    pos_t = pos[...].astype(F32).T
    lane = lax.broadcasted_iota(jnp.int32, (128, 128), 1)
    for i in range(8):
        at = pos_t[:, i:i + 1]
        angle = at * freq[...]
        rows = pl.ds(i * 128, 128)
        cosb[rows, :] = jnp.cos(angle)
        sinb[rows, :] = jnp.where(lane < 64, -1.0, 1.0) * jnp.sin(angle)
        row = lax.broadcasted_iota(jnp.int32, (128, 128), 0) + i * 128
        startb[rows, :] = row - at.astype(jnp.int32)
    up_lo.wait_recv()
    r_up = s3_send(wq.at[g, lo, ym], updev)
    dn_hi.wait_recv()
    r_dn = s3_send(wq.at[g, hi, yp], dndev)
    z_lo.wait_recv()
    up_tlo = s3_send(wq.at[g2, lo, y], updev)
    z_hi.wait_recv()
    dn_thi = s3_send(wq.at[g2, hi, y], dndev)
    up_thi = s3_send(wq.at[g2, hi, y], updev)
    dn_tlo = s3_send(wq.at[g2, lo, y], dndev)
    sib_b.append(s3_send(wq.at[g2, :, y], sib))
    w_wait(2, 1)
    v_send(2, (1, 2, 3))
    w_share(2, 0)
    up_hi.wait_recv()
    sib_a.append(s3_send(wq.at[g, :, ym], sib))
    dn_lo.wait_recv()
    sib_a.append(s3_send(wq.at[g, :, yp], sib))
    v_relay(0, (1, 2, 3))
    r_up.wait_recv()
    r_dn.wait_recv()
    sib_a.append(s3_send(wq.at[g, :, y2], sib))
    up_tlo.wait_recv()
    r_tup = s3_send(wq.at[g2, lo, ym], updev)
    dn_thi.wait_recv()
    r_tdn = s3_send(wq.at[g2, hi, yp], dndev)
    v_relay(2, (1, 2, 3))
    w_wait(1, 1)
    v_send(1, (0, 1, 2, 3))
    w_share(1, 0)
    for cp in sib_a:
        cp.wait_recv()

    def project(i, which):
        rows = pl.ds(i * CHUNK, CHUNK)
        weights = jnp.concatenate([wq[which].reshape(D, 128), wq[2 + which].reshape(D, 128)], axis=1)
        p = jnp.dot(normed[rows, :], weights, preferred_element_type=F32)
        cos, sin = cosb[rows, :], sinb[rows, :]

        def rotate(u):
            return u * cos + pltpu.roll(u, 64, 1) * sin

        qb[which, rows, :] = (rotate(p[:, :128]) * QUERY_SCALE).astype(BF16)
        u = p[:, 128:]
        kv[which, rows, :] = jnp.where(which == 0, rotate(u), u).astype(BF16)

    project(0, zl)
    up_thi.wait_recv()
    sib_b.append(s3_send(wq.at[g2, :, ym], sib))
    dn_tlo.wait_recv()
    sib_b.append(s3_send(wq.at[g2, :, yp], sib))
    project(1, zl)
    project(2, zl)
    project(3, zl)
    r_tup.wait_recv()
    r_tdn.wait_recv()
    sib_b.append(s3_send(wq.at[g2, :, y2], sib))
    for cp in sib_b:
        cp.wait_recv()

    def attend(i):
        rows = pl.ds(i * CHUNK, CHUNK)
        n = (i + 1) * CHUNK
        first = startb[rows, 0:1]
        at = lax.broadcasted_iota(jnp.int32, (CHUNK, n), 1)
        row = lax.broadcasted_iota(jnp.int32, (CHUNK, n), 0) + i * CHUNK
        allowed = (at <= row) & (at >= first)
        for j in range(2):
            s = lax.dot_general(qb[j, rows, :], kv[0, 0:n, :], NT, preferred_element_type=F32)
            s = jnp.where(allowed, s, -1e30)
            e = jnp.exp(s - jnp.max(s, axis=1, keepdims=True))
            a = (e * (1.0 / jnp.sum(e, axis=1, keepdims=True))).astype(BF16)
            hs[i][zh, x, j] = jnp.dot(a, kv[1, 0:n, :], preferred_element_type=F32).astype(BF16)

    zpair = (rep, (tp + 4) % 8)
    xup, xdn = shifted("x", 1), shifted("x", -1)
    oz = 1 - zh
    top, bot = pl.ds(0, CHUNK // 2), pl.ds(CHUNK // 2, CHUNK // 2)
    h_in = [dict() for _ in range(N_CHUNK)]

    def h_send(i, name, block, dev):
        k = len(h_in[i])
        h_in[i][name] = go(remote(block, block, h_ss.at[i, k], h_rs.at[i, k], dev))

    def h_got(i, name):
        h_in[i][name].wait_recv()

    def h_stage(i, stage):
        h = hs[i]
        if stage == 0:
            h_send(i, "z0", h.at[zh, x, 0], zpair)
            h_send(i, "u1t", h.at[zh, x, 1, top], xup)
            h_send(i, "d1b", h.at[zh, x, 1, bot], xdn)
            h_send(i, "u1b", h.at[zh, x, 1, bot], xup)
            h_send(i, "d1t", h.at[zh, x, 1, top], xdn)
            h_send(i, "u0t", h.at[zh, x, 0, top], xup)
            h_send(i, "d0b", h.at[zh, x, 0, bot], xdn)
            h_send(i, "u0b", h.at[zh, x, 0, bot], xup)
            h_send(i, "d0t", h.at[zh, x, 0, top], xdn)
            h_send(i, "z1", h.at[zh, x, 1], zpair)
        elif stage == 1:
            h_got(i, "u1t")
            h_send(i, "ru1", h.at[zh, xm, 1, top], xup)
            h_got(i, "d1b")
            h_send(i, "rd1", h.at[zh, xp, 1, bot], xdn)
            h_got(i, "z0")
            h_send(i, "v0t", h.at[oz, x, 0, top], xup)
            h_send(i, "e0b", h.at[oz, x, 0, bot], xdn)
            h_send(i, "v0b", h.at[oz, x, 0, bot], xup)
            h_send(i, "e0t", h.at[oz, x, 0, top], xdn)
            h_got(i, "u1b")
            h_send(i, "zm", h.at[zh, xm, 1], zpair)
            h_got(i, "d1t")
            h_send(i, "zp", h.at[zh, xp, 1], zpair)
        elif stage == 2:
            h_got(i, "u0t")
            h_send(i, "ru0", h.at[zh, xm, 0, top], xup)
            h_got(i, "d0b")
            h_send(i, "rd0", h.at[zh, xp, 0, bot], xdn)
            h_got(i, "ru1")
            h_got(i, "rd1")
            h_send(i, "z2", h.at[zh, x2, 1], zpair)
            h_got(i, "v0t")
            h_send(i, "rv0", h.at[oz, xm, 0, top], xup)
            h_got(i, "e0b")
            h_send(i, "re0", h.at[oz, xp, 0, bot], xdn)
        else:
            for name in ("u0b", "d0t", "v0b", "e0t", "z1", "zm", "zp", "z2", "ru0", "rd0", "rv0", "re0"):
                h_got(i, name)

    def heads_of(i):
        project(i, 1 - zl)
        attend(i)
        h_stage(i, 0)

    heads_of(0)
    heads_of(1)
    h_stage(0, 1)
    heads_of(2)
    v_relay(1, (0, 1, 2, 3))
    h_stage(0, 2)
    h_stage(1, 1)
    project(3, 1 - zl)
    attend(3)
    h_stage(3, 0)
    h_stage(0, 3)
    h_stage(1, 2)
    h_stage(2, 1)

    every = (y, yp, ym, y2)

    def out_proj(p, i, ys=every):
        rows = pl.ds(i * CHUNK, CHUNK)
        n = W_N[p]
        far = len(ys) == 1
        left = []
        for at in ys:
            for z_at in range(2):
                for c_at in range(2):
                    b = smap[z_at * 8 + at * 2 + c_at]
                    left.append(hs[i][b // 8, (b // 2) % 4, b % 2])
        left = jnp.concatenate(left, axis=1)
        squares = jnp.zeros((CHUNK, 1), F32)
        for half in range(2):
            right = jnp.concatenate(
                [
                    ws[p][half * 2 + z_at, at, c_at].reshape(4 * n, 128)
                    for at in ys for z_at in range(2) for c_at in range(2)
                ],
                axis=1,
            )
            t = lax.dot_general(left, right, NT, preferred_element_type=F32)
            for k in range(2):
                base = half * 2304 + k * 1152
                for odd in range(2):
                    u = t[:, (2 * k + odd) * n:(2 * k + odd + 1) * n]
                    if p == 0:
                        if odd:
                            continue
                        u = t[:, 2 * k * n:2 * (k + 1) * n]
                    cols = slice(base + W_COL[p][odd], base + W_COL[p][odd] + u.shape[1])
                    if far:
                        u = u + normed[rows, cols].astype(F32)
                    if len(ys) != 3:
                        squares = squares + jnp.sum(u * u, axis=1, keepdims=True)
                    normed[rows, cols] = u.astype(BF16)
        if len(ys) != 3:
            squares = jnp.broadcast_to(squares, (CHUNK, 128))
            total[rows, :] = squares if p == 0 else total[rows, :] + squares

    def finish(i):
        rows = pl.ds(i * CHUNK, CHUNK)
        scale = lax.rsqrt(total[rows, 0:1] * (1.0 / D) + EPS)
        o_ref[rows, :] = (
            o_ref[rows, :].astype(F32) + normed[rows, :].astype(F32) * scale * gain2[...]
        ).astype(BF16)

    near = (y, yp, ym)
    w_near(0)
    w_far(0)
    h_stage(3, 1)
    w_ready(0)
    out_proj(0, 0)
    h_stage(2, 2)
    w_near(2)
    w_far(2)
    h_stage(1, 3)
    out_proj(0, 1)
    h_stage(3, 2)
    w_ready(2)
    out_proj(2, 0)
    out_proj(2, 1)
    w_near(1)
    h_stage(2, 3)
    out_proj(0, 2)
    out_proj(2, 2)
    w_ready(1, 0, 3)
    for i in range(3):
        out_proj(1, i, near)
    h_stage(3, 3)
    out_proj(0, 3)
    out_proj(2, 3)
    w_far(1)
    out_proj(1, 3, near)
    w_ready(1, 3)
    for i in range(N_CHUNK):
        out_proj(1, i, (y2,))
        finish(i)

    lax.fori_loop(1, 8, lambda d, _: (s1_copy(d).wait_send(), 0)[1], 0)
    lax.fori_loop(1, 8, lambda d, _: (s2_copy(d).wait_send(), 0)[1], 0)
    for cp in started:
        cp.wait_send()


def on_device(tokens, gain_pre, gain_post, qkv_shards, out_shards, shard_map, positions):
    freq = np.exp(np.arange(64) * (-2.0 * math.log(10000.0) / HDIM)).astype(np.float32)
    freq = jnp.asarray(np.concatenate([freq, freq])[None])
    vmem, hbm = pl.BlockSpec(memory_space=pltpu.VMEM), pl.BlockSpec(memory_space=pl.ANY)
    smem = pl.BlockSpec(memory_space=pltpu.SMEM)
    sem = pltpu.SemaphoreType.DMA
    heads = pltpu.VMEM((2, 4, 2, CHUNK, 128), BF16)
    return pl.pallas_call(
        kernel,
        name="attention_block",
        out_shape=pltpu.VMEM((TOK, D), BF16),
        in_specs=[hbm, vmem, vmem, vmem, hbm, hbm, smem, vmem],
        out_specs=vmem,
        scratch_shapes=[
            pltpu.VMEM((8, 2, PART, 128), BF16),
            pltpu.VMEM((8, PART, 128), BF16),
            pltpu.VMEM((4, 8, 4, PART, 128), BF16),
            *[pltpu.VMEM((4, 4, 2, 4, n, 128), BF16) for n in W_N],
            heads, heads, heads, heads,
            pltpu.VMEM((TOK, D), BF16),
            pltpu.VMEM((2, TOK, 128), BF16),
            pltpu.VMEM((2, TOK, 128), BF16),
            pltpu.VMEM((TOK, 128), F32),
            pltpu.VMEM((TOK, 128), F32),
            pltpu.VMEM((TOK, 128), jnp.int32),
            pltpu.VMEM((TOK, 128), F32),
            pltpu.VMEM((1, D), F32),
            pltpu.VMEM((1, D), F32),
            sem((8,)), sem((8,)), sem((8,)), sem((8,)), sem((32,)), sem((32,)),
            sem((3, 4, 4)), sem((3, 4, 4)), sem((3, 4, 6)), sem((3, 4, 6)), sem((4, 24)), sem((4, 24)), sem((12,)),
        ],
        compiler_params=pltpu.CompilerParams(
            collective_id=0, has_side_effects=True, vmem_limit_bytes=52 << 20
        ),
        cost_estimate=pl.CostEstimate(flops=26 * 10**9, bytes_accessed=30 * 10**6, transcendentals=3 * 10**6),
    )(
        tokens, gain_pre.reshape(D // 128, 128), gain_post.reshape(D // 128, 128), freq, qkv_shards, jnp.swapaxes(out_shards, 1, 2),
        shard_map, positions.reshape(8, 128),
    )


def solution(mesh):
    placed = (P("rep", None), P(), P(), P("rep", "tp", None), P("rep", None, "tp"), P(), P("rep"))
    return jax.shard_map(
        on_device, mesh=mesh, in_specs=placed, out_specs=P("rep", None), check_vma=False
    )
```

```python
import math

import jax
import jax.numpy as jnp
import numpy as np
from jax import lax
from jax.experimental import pallas as pl
from jax.experimental.pallas import tpu as pltpu
from jax.sharding import PartitionSpec as P

D = 4608
TOK = 1024
HDIM = 128
CHUNK = 256
N_CHUNK = TOK // CHUNK
SEG = 576
PART = 144
QUERY_SCALE = 1.0 / 12.0
EPS = 1e-06
MESH = pl.DeviceIdType.MESH
F32 = jnp.float32
BF16 = jnp.bfloat16
NT = (((1,), (1,)), ((), ()))
W_N = (192, 256, 128)
W_OFF = ((384, 0), (0, 320), (256, 192))
W_ORDER = ("zyx", "xzy", "yxz")
W_COL = ((384, 576), (0, 896), (256, 768))


def device(x, y, z, c):
    return ((z % 2) * 8 + y * 2 + c, (z // 2) * 4 + x)


def kernel(
    tok, gpre, gpost, freq, qkv, outs, smap, pos, o_ref,
    s1, send2, wq, wa, wb, wc, h0, h1, h2, h3, normed, qb, kv, cosb, sinb, startb, total, gain1, gain2,
    s1_ss, s1_rs, s2_ss, s2_rs, s3_ss, s3_rs, w_ss, w_rs, v_ss, v_rs, h_ss, h_rs, loc,
):
    hs = (h0, h1, h2, h3)
    ws = (wa, wb, wc)
    rep = lax.axis_index("rep")
    tp = lax.axis_index("tp")
    c, y, zl = rep % 2, (rep // 2) % 4, rep // 8
    x, zh = tp % 4, tp // 4
    z = zh * 2 + zl
    yp, ym, y2 = (y + 1) % 4, (y + 3) % 4, (y + 2) % 4
    xp, xm, x2 = (x + 1) % 4, (x + 3) % 4, (x + 2) % 4
    full = slice(None)

    def shifted(axis, by):
        at = {"x": x, "y": y, "z": z}
        at[axis] = (at[axis] + by + 4) % 4
        return device(at["x"], at["y"], at["z"], c)

    def remote(src, dst, ss, rs, dev):
        return pltpu.make_async_remote_copy(
            src_ref=src, dst_ref=dst, send_sem=ss, recv_sem=rs, device_id=dev, device_id_type=MESH
        )

    started = []

    def go(cp):
        cp.start()
        started.append(cp)
        return cp

    tok_copies = []
    for i in range(N_CHUNK):
        rows = pl.ds(i * CHUNK, CHUNK)
        cp = pltpu.make_async_copy(tok.at[rows], o_ref.at[rows], loc.at[i])
        cp.start()
        tok_copies.append(cp)
    w_own = []
    for p in range(3):
        off = pl.multiple_of(jnp.where(x % 2 == 0, W_OFF[p][0], W_OFF[p][1]), 64)
        cp = pltpu.make_async_copy(outs.at[0, pl.ds(off, W_N[p])], ws[p].at[z, y, c, x], loc.at[6 + p])
        cp.start()
        w_own.append(cp)

    barrier = pltpu.get_barrier_semaphore()

    def greet_rep(d, _):
        pl.semaphore_signal(barrier, inc=1, device_id=((rep + d) % 16, tp), device_id_type=MESH)
        return 0

    def greet_tp(d, _):
        pl.semaphore_signal(barrier, inc=1, device_id=(rep, (tp + d) % 8), device_id_type=MESH)
        return 0

    lax.fori_loop(1, 16, greet_rep, 0)
    lax.fori_loop(1, 8, greet_tp, 0)
    far = jnp.where(zl == 0, 3, 1)
    pl.semaphore_signal(barrier, inc=1, device_id=device(x, y, (z + far) % 4, c), device_id_type=MESH)
    pl.semaphore_wait(barrier, 23)

    place = rep // 2
    sib = (rep + 1 - 2 * c, tp)

    def s1_src(to):
        rows = pl.ds(pl.multiple_of((to % 4) * PART, 16), PART)
        cols = pl.ds(pl.multiple_of((to // 4) * 128, 128), 128)
        return qkv.at[0, rows, cols]

    own1 = pltpu.make_async_copy(s1_src(place), s1.at[place, c], loc.at[4])
    own1.start()

    def s1_copy(d):
        to = (place + d) % 8
        return remote(s1_src(to), s1.at[place, c], s1_ss.at[d], s1_rs.at[d], (to * 2 + c, tp))

    lax.fori_loop(1, 8, lambda d, _: (s1_copy(d).start(), 0)[1], 0)

    def w_set(p, done, axis=None, by=0, half=None):
        at = {"x": x, "y": y, "z": z}
        if axis is not None:
            at[axis] = (at[axis] + by + 4) % 4
        n = W_N[p]
        rows = pl.ds(0, n) if half is None else pl.ds(half * (n // 2), n // 2)
        iz, iy, ix = (full if a in done else at[a] for a in "zyx")
        return ws[p].at[iz, iy, c, ix, rows]

    w_in = {}

    def w_send(p, step):
        axis, done = W_ORDER[p][step], W_ORDER[p][:step]
        cps = []
        for k, by in enumerate((1, -1, 2)):
            block = w_set(p, done)
            cps.append(go(remote(block, block, w_ss.at[p, step, k], w_rs.at[p, step, k], shifted(axis, by))))
        w_in[p, step] = cps

    def w_wait(p, step):
        for cp in w_in[p, step]:
            cp.wait_recv()

    ways = ((1, 0), (-1, 1), (1, 1), (-1, 0))
    v_in = {}

    def v_block(p, q, by, half):
        first, second, last = W_ORDER[p]
        at = {"x": x, "y": y, "z": z}
        at[second] = (at[second] + (0, 1, 3, 2)[q]) % 4
        at[last] = (at[last] + by + 4) % 4
        at[first] = full
        n = W_N[p] // 2
        return ws[p].at[at["z"], at["y"], c, at["x"], pl.ds(half * n, n)]

    def v_send(p, qs):
        for k, (by, half) in enumerate(ways):
            for q in qs:
                block = v_block(p, q, 0, half)
                cp = remote(block, block, v_ss.at[p, q, k], v_rs.at[p, q, k], shifted(W_ORDER[p][2], by))
                v_in[p, q, k] = go(cp)

    def v_relay(p, qs):
        for k in range(2):
            by, half = ways[k]
            for q in qs:
                v_in[p, q, k].wait_recv()
                block = v_block(p, q, -by, half)
                cp = remote(block, block, v_ss.at[p, q, 4 + k], v_rs.at[p, q, 4 + k], shifted(W_ORDER[p][2], by))
                v_in[p, q, 4 + k] = go(cp)

    w_sib = {0: [], 1: [], 2: []}

    def w_share(p, by):
        axis, done = W_ORDER[p][2], W_ORDER[p][:2]
        k = len(w_sib[p])
        block = w_set(p, done, axis, by)
        w_sib[p].append(go(remote(block, block, w_ss.at[p, 3, k], w_rs.at[p, 3, k], sib)))

    def w_near(p):
        for q in range(4):
            v_in[p, q, 2].wait_recv()
            v_in[p, q, 3].wait_recv()
        w_share(p, 1)
        w_share(p, -1)

    def w_far(p):
        for q in range(4):
            v_in[p, q, 4].wait_recv()
            v_in[p, q, 5].wait_recv()
        w_share(p, 2)

    def w_ready(p, first=0, last=4):
        for cp in w_sib[p][first:last]:
            cp.wait_recv()

    for cp in w_own:
        cp.wait()
    for p in range(3):
        w_send(p, 0)

    for k in range(D // 128):
        gain1[:, k * 128:(k + 1) * 128] = gpre[k:k + 1, :]
        gain2[:, k * 128:(k + 1) * 128] = gpost[k:k + 1, :]

    def norm_rows(i, _):
        rows = pl.ds(pl.multiple_of(i * 32, 32), 32)
        v = o_ref[rows, :].astype(F32)
        ms = jnp.sum(v * v, axis=1, keepdims=True) * (1.0 / D)
        normed[rows, :] = (v * lax.rsqrt(ms + EPS) * gain1[...]).astype(BF16)
        return 0

    for cp in tok_copies:
        cp.wait()
    lax.fori_loop(0, 8, norm_rows, 0)
    w_wait(0, 0)
    w_send(0, 1)
    v_send(0, (0,))
    w_wait(2, 0)
    v_send(2, (0,))
    lax.fori_loop(8, 14, norm_rows, 0)
    lax.fori_loop(1, 8, lambda d, _: (s1_copy(d).wait_recv(), 0)[1], 0)
    own1.wait()
    swap = go(remote(s1.at[:, c], s1.at[:, c], s1_ss.at[0], s1_rs.at[0], sib))
    lax.fori_loop(14, 22, norm_rows, 0)
    swap.wait_recv()

    def order_of(b):
        at = jnp.int32(0)
        for s in range(16):
            at = jnp.where(smap[s] == b, s, at)
        return at

    for t in range(8):
        at = order_of(2 * t + c)
        send2[t] = s1[at // 2, at % 2]
    g = c * 2 + zl
    g2 = c * 2 + (1 - zl)

    own2 = pltpu.make_async_copy(send2.at[tp], wq.at[g, tp, y], loc.at[5])
    own2.start()

    def s2_copy(d):
        to = (tp + d) % 8
        return remote(send2.at[to], wq.at[g, tp, y], s2_ss.at[d], s2_rs.at[d], (rep, to))

    lax.fori_loop(1, 8, lambda d, _: (s2_copy(d).start(), 0)[1], 0)
    v_relay(0, (0,))
    w_send(2, 1)
    v_relay(2, (0,))
    w_wait(1, 0)
    lax.fori_loop(22, 32, norm_rows, 0)

    lax.fori_loop(1, 8, lambda d, _: (s2_copy(d).wait_recv(), 0)[1], 0)
    own2.wait()

    zdev = ((1 - zl) * 8 + y * 2 + c, tp)
    updev, dndev = shifted("y", 1), shifted("y", -1)
    lo, hi = pl.ds(0, 4), pl.ds(4, 4)
    k3 = [0]

    def s3_send(block, dev):
        k = k3[0]
        k3[0] += 1
        return go(remote(block, block, s3_ss.at[k], s3_rs.at[k], dev))

    z_lo = s3_send(wq.at[g, lo, y], zdev)
    up_lo = s3_send(wq.at[g, lo, y], updev)
    dn_hi = s3_send(wq.at[g, hi, y], dndev)
    z_hi = s3_send(wq.at[g, hi, y], zdev)
    up_hi = s3_send(wq.at[g, hi, y], updev)
    dn_lo = s3_send(wq.at[g, lo, y], dndev)
    sib_a = [s3_send(wq.at[g, :, y], sib)]
    sib_b = []
    w_send(1, 1)
    w_wait(0, 1)
    v_send(0, (1, 2, 3))
    w_share(0, 0)
    pos_t = pos[...].astype(F32).T
    lane = lax.broadcasted_iota(jnp.int32, (128, 128), 1)
    for i in range(8):
        at = pos_t[:, i:i + 1]
        angle = at * freq[...]
        rows = pl.ds(i * 128, 128)
        cosb[rows, :] = jnp.cos(angle)
        sinb[rows, :] = jnp.where(lane < 64, -1.0, 1.0) * jnp.sin(angle)
        row = lax.broadcasted_iota(jnp.int32, (128, 128), 0) + i * 128
        startb[rows, :] = row - at.astype(jnp.int32)
    up_lo.wait_recv()
    r_up = s3_send(wq.at[g, lo, ym], updev)
    dn_hi.wait_recv()
    r_dn = s3_send(wq.at[g, hi, yp], dndev)
    z_lo.wait_recv()
    up_tlo = s3_send(wq.at[g2, lo, y], updev)
    z_hi.wait_recv()
    dn_thi = s3_send(wq.at[g2, hi, y], dndev)
    up_thi = s3_send(wq.at[g2, hi, y], updev)
    dn_tlo = s3_send(wq.at[g2, lo, y], dndev)
    sib_b.append(s3_send(wq.at[g2, :, y], sib))
    w_wait(2, 1)
    v_send(2, (1, 2, 3))
    w_share(2, 0)
    up_hi.wait_recv()
    sib_a.append(s3_send(wq.at[g, :, ym], sib))
    dn_lo.wait_recv()
    sib_a.append(s3_send(wq.at[g, :, yp], sib))
    v_relay(0, (1, 2, 3))
    r_up.wait_recv()
    r_dn.wait_recv()
    sib_a.append(s3_send(wq.at[g, :, y2], sib))
    up_tlo.wait_recv()
    r_tup = s3_send(wq.at[g2, lo, ym], updev)
    dn_thi.wait_recv()
    r_tdn = s3_send(wq.at[g2, hi, yp], dndev)
    v_relay(2, (1, 2, 3))
    w_wait(1, 1)
    v_send(1, (0, 1, 2, 3))
    w_share(1, 0)
    for cp in sib_a:
        cp.wait_recv()

    def project(i, which):
        rows = pl.ds(i * CHUNK, CHUNK)
        weights = jnp.concatenate([wq[which].reshape(D, 128), wq[2 + which].reshape(D, 128)], axis=1)
        p = jnp.dot(normed[rows, :], weights, preferred_element_type=F32)
        cos, sin = cosb[rows, :], sinb[rows, :]

        def rotate(u):
            return u * cos + pltpu.roll(u, 64, 1) * sin

        qb[which, rows, :] = (rotate(p[:, :128]) * QUERY_SCALE).astype(BF16)
        u = p[:, 128:]
        kv[which, rows, :] = jnp.where(which == 0, rotate(u), u).astype(BF16)

    project(0, zl)
    up_thi.wait_recv()
    sib_b.append(s3_send(wq.at[g2, :, ym], sib))
    dn_tlo.wait_recv()
    sib_b.append(s3_send(wq.at[g2, :, yp], sib))
    project(1, zl)
    project(2, zl)
    project(3, zl)
    r_tup.wait_recv()
    r_tdn.wait_recv()
    sib_b.append(s3_send(wq.at[g2, :, y2], sib))
    for cp in sib_b:
        cp.wait_recv()

    def attend(i):
        rows = pl.ds(i * CHUNK, CHUNK)
        n = (i + 1) * CHUNK
        first = startb[rows, 0:1]
        at = lax.broadcasted_iota(jnp.int32, (CHUNK, n), 1)
        row = lax.broadcasted_iota(jnp.int32, (CHUNK, n), 0) + i * CHUNK
        allowed = (at <= row) & (at >= first)
        for j in range(2):
            s = lax.dot_general(qb[j, rows, :], kv[0, 0:n, :], NT, preferred_element_type=F32)
            s = jnp.where(allowed, s, -1e30)
            e = jnp.exp(s - jnp.max(s, axis=1, keepdims=True))
            a = (e * (1.0 / jnp.sum(e, axis=1, keepdims=True))).astype(BF16)
            hs[i][zh, x, j] = jnp.dot(a, kv[1, 0:n, :], preferred_element_type=F32).astype(BF16)

    zpair = (rep, (tp + 4) % 8)
    xup, xdn = shifted("x", 1), shifted("x", -1)
    oz = 1 - zh
    top, bot = pl.ds(0, CHUNK // 2), pl.ds(CHUNK // 2, CHUNK // 2)
    h_in = [dict() for _ in range(N_CHUNK)]

    def h_send(i, name, block, dev):
        k = len(h_in[i])
        h_in[i][name] = go(remote(block, block, h_ss.at[i, k], h_rs.at[i, k], dev))

    def h_got(i, name):
        h_in[i][name].wait_recv()

    def h_stage(i, stage):
        h = hs[i]
        if stage == 0:
            h_send(i, "z0", h.at[zh, x, 0], zpair)
            h_send(i, "u1t", h.at[zh, x, 1, top], xup)
            h_send(i, "d1b", h.at[zh, x, 1, bot], xdn)
            h_send(i, "u1b", h.at[zh, x, 1, bot], xup)
            h_send(i, "d1t", h.at[zh, x, 1, top], xdn)
            h_send(i, "u0t", h.at[zh, x, 0, top], xup)
            h_send(i, "d0b", h.at[zh, x, 0, bot], xdn)
            h_send(i, "u0b", h.at[zh, x, 0, bot], xup)
            h_send(i, "d0t", h.at[zh, x, 0, top], xdn)
            h_send(i, "z1", h.at[zh, x, 1], zpair)
        elif stage == 1:
            h_got(i, "u1t")
            h_send(i, "ru1", h.at[zh, xm, 1, top], xup)
            h_got(i, "d1b")
            h_send(i, "rd1", h.at[zh, xp, 1, bot], xdn)
            h_got(i, "z0")
            h_send(i, "v0t", h.at[oz, x, 0, top], xup)
            h_send(i, "e0b", h.at[oz, x, 0, bot], xdn)
            h_send(i, "v0b", h.at[oz, x, 0, bot], xup)
            h_send(i, "e0t", h.at[oz, x, 0, top], xdn)
            h_got(i, "u1b")
            h_send(i, "zm", h.at[zh, xm, 1], zpair)
            h_got(i, "d1t")
            h_send(i, "zp", h.at[zh, xp, 1], zpair)
        elif stage == 2:
            h_got(i, "u0t")
            h_send(i, "ru0", h.at[zh, xm, 0, top], xup)
            h_got(i, "d0b")
            h_send(i, "rd0", h.at[zh, xp, 0, bot], xdn)
            h_got(i, "ru1")
            h_got(i, "rd1")
            h_send(i, "z2", h.at[zh, x2, 1], zpair)
            h_got(i, "v0t")
            h_send(i, "rv0", h.at[oz, xm, 0, top], xup)
            h_got(i, "e0b")
            h_send(i, "re0", h.at[oz, xp, 0, bot], xdn)
        else:
            for name in ("u0b", "d0t", "v0b", "e0t", "z1", "zm", "zp", "z2", "ru0", "rd0", "rv0", "re0"):
                h_got(i, name)

    def heads_of(i):
        project(i, 1 - zl)
        attend(i)
        h_stage(i, 0)

    heads_of(0)
    heads_of(1)
    h_stage(0, 1)
    heads_of(2)
    v_relay(1, (0, 1, 2, 3))
    h_stage(0, 2)
    h_stage(1, 1)
    project(3, 1 - zl)
    attend(3)
    h_stage(3, 0)
    h_stage(0, 3)
    h_stage(1, 2)
    h_stage(2, 1)

    every = (y, yp, ym, y2)

    def out_proj(p, i, ys=every):
        rows = pl.ds(i * CHUNK, CHUNK)
        n = W_N[p]
        far = len(ys) == 1
        spots = [(at, z_at, c_at) for at in ys for z_at in range(2) for c_at in range(2)]

        def one_half(half, squares):
            left = []
            for at, z_at, c_at in spots:
                b = smap[z_at * 8 + at * 2 + c_at]
                left.append(hs[i][b // 8, (b // 2) % 4, b % 2])
            left = jnp.concatenate(left, axis=1)
            right = jnp.concatenate(
                [ws[p][half * 2 + z_at, at, c_at].reshape(4 * n, 128) for at, z_at, c_at in spots], axis=1
            )
            t = lax.dot_general(left, right, NT, preferred_element_type=F32)
            for k in range(2):
                for odd in range(2):
                    u = t[:, (2 * k + odd) * n:(2 * k + odd + 1) * n]
                    if p == 0:
                        if odd:
                            continue
                        u = t[:, 2 * k * n:2 * (k + 1) * n]
                    start = pl.multiple_of(half * 2304 + k * 1152 + W_COL[p][odd], 128)
                    cols = pl.ds(start, u.shape[1])
                    if far:
                        u = u + normed[rows, cols].astype(F32)
                    if len(ys) != 3:
                        squares = squares + jnp.sum(u * u, axis=1, keepdims=True)
                    normed[rows, cols] = u.astype(BF16)
            return squares

        squares = lax.fori_loop(0, 2, one_half, jnp.zeros((CHUNK, 1), F32))
        if len(ys) != 3:
            squares = jnp.broadcast_to(squares, (CHUNK, 128))
            total[rows, :] = squares if p == 0 else total[rows, :] + squares

    def finish(i):
        rows = pl.ds(i * CHUNK, CHUNK)
        scale = lax.rsqrt(total[rows, 0:1] * (1.0 / D) + EPS)
        o_ref[rows, :] = (
            o_ref[rows, :].astype(F32) + normed[rows, :].astype(F32) * scale * gain2[...]
        ).astype(BF16)

    near = (y, yp, ym)
    w_near(0)
    w_far(0)
    h_stage(3, 1)
    w_ready(0)
    out_proj(0, 0)
    h_stage(2, 2)
    w_near(2)
    w_far(2)
    h_stage(1, 3)
    out_proj(0, 1)
    h_stage(3, 2)
    w_ready(2)
    out_proj(2, 0)
    out_proj(2, 1)
    w_near(1)
    h_stage(2, 3)
    out_proj(0, 2)
    out_proj(2, 2)
    w_ready(1, 0, 3)
    for i in range(3):
        out_proj(1, i, near)
    h_stage(3, 3)
    out_proj(0, 3)
    out_proj(2, 3)
    w_far(1)
    out_proj(1, 3, near)
    w_ready(1, 3)
    for i in range(N_CHUNK):
        out_proj(1, i, (y2,))
        finish(i)

    lax.fori_loop(1, 8, lambda d, _: (s1_copy(d).wait_send(), 0)[1], 0)
    lax.fori_loop(1, 8, lambda d, _: (s2_copy(d).wait_send(), 0)[1], 0)
    for cp in started:
        cp.wait_send()


def on_device(tokens, gain_pre, gain_post, qkv_shards, out_shards, shard_map, positions):
    freq = np.exp(np.arange(64) * (-2.0 * math.log(10000.0) / HDIM)).astype(np.float32)
    freq = jnp.asarray(np.concatenate([freq, freq])[None])
    vmem, hbm = pl.BlockSpec(memory_space=pltpu.VMEM), pl.BlockSpec(memory_space=pl.ANY)
    smem = pl.BlockSpec(memory_space=pltpu.SMEM)
    sem = pltpu.SemaphoreType.DMA
    heads = pltpu.VMEM((2, 4, 2, CHUNK, 128), BF16)
    return pl.pallas_call(
        kernel,
        name="attention_block",
        out_shape=pltpu.VMEM((TOK, D), BF16),
        in_specs=[hbm, vmem, vmem, vmem, hbm, hbm, smem, vmem],
        out_specs=vmem,
        scratch_shapes=[
            pltpu.VMEM((8, 2, PART, 128), BF16),
            pltpu.VMEM((8, PART, 128), BF16),
            pltpu.VMEM((4, 8, 4, PART, 128), BF16),
            *[pltpu.VMEM((4, 4, 2, 4, n, 128), BF16) for n in W_N],
            heads, heads, heads, heads,
            pltpu.VMEM((TOK, D), BF16),
            pltpu.VMEM((2, TOK, 128), BF16),
            pltpu.VMEM((2, TOK, 128), BF16),
            pltpu.VMEM((TOK, 128), F32),
            pltpu.VMEM((TOK, 128), F32),
            pltpu.VMEM((TOK, 128), jnp.int32),
            pltpu.VMEM((TOK, 128), F32),
            pltpu.VMEM((1, D), F32),
            pltpu.VMEM((1, D), F32),
            sem((8,)), sem((8,)), sem((8,)), sem((8,)), sem((32,)), sem((32,)),
            sem((3, 4, 4)), sem((3, 4, 4)), sem((3, 4, 6)), sem((3, 4, 6)), sem((4, 24)), sem((4, 24)), sem((12,)),
        ],
        compiler_params=pltpu.CompilerParams(
            collective_id=0, has_side_effects=True, vmem_limit_bytes=52 << 20
        ),
        cost_estimate=pl.CostEstimate(flops=26 * 10**9, bytes_accessed=30 * 10**6, transcendentals=3 * 10**6),
    )(
        tokens, gain_pre.reshape(D // 128, 128), gain_post.reshape(D // 128, 128), freq, qkv_shards, jnp.swapaxes(out_shards, 1, 2),
        shard_map, positions.reshape(8, 128),
    )


def solution(mesh):
    placed = (P("rep", None), P(), P(), P("rep", "tp", None), P("rep", None, "tp"), P(), P("rep"))
    return jax.shard_map(
        on_device, mesh=mesh, in_specs=placed, out_specs=P("rep", None), check_vma=False
    )
```
